256 devices in a mesh: chain: 16 (over y, x), sector: 16 (over z, core).
Axes of the slice: x: 4, y: 4, z: 8, core: 2. Of those that a mesh axis runs over, the one named last changes fastest.
Arguments:
- left_edge: float32 [16, 14, 128, 128], P('sector'), may hold values from -0.5 to 0.5
- transfer: float32 [16, 16, 128, 128], P('chain', 'sector'), may hold values from -0.078125 to 0.078125
- completed: float32 [16, 16, 14, 128, 128], P('chain', 'sector'), may hold values from -0.25 to 0.25
- right_env: bfloat16 [16, 16, 14, 128, 128], P('chain', 'sector'), may hold values from -0.5 to 0.5
- psi_init: bfloat16 [16, 16, 16, 128, 128], P('chain', 'sector'), may hold values from -6 to 6
- mpo: bfloat16 [14, 16, 16, 14], replicated, may hold values from -0.75 to 0.75
- mpo_mask: int32 [14, 14], replicated, may hold values 0 or 1
- charge_shift: int32 [16, 16], P('sector'), may hold values from -1 to 1
- block_size: int32 [16], replicated, may hold values from 1 to 128, 1536 in all
Outputs:
- psi_out: bfloat16 [16, 16, 16, 128, 128], P('chain', 'sector')
- energy: float32 [16], P('chain')
The draws below stay inside these ranges and needn't reach their ends.
Inputs may be any that keep to these rules, and one draw needn't show every extreme that they name: `block_size`: some block has 128 live rows.
All inputs are finite; a program needn't handle non-finite values.
Results may differ from the reference program's by a relative error of at most 0.024.
Values may be sent and summed in bfloat16 or wider, within the bound.
No kernel may reach another device: no remote copies, remote signals or barrier semaphores. Data moves between devices by JAX's collectives and lax.ppermute only.
A program may use at most 128 MiB of HBM per device.

```python
import math
import jax
import jax.numpy as jnp
import numpy as np
from jax import lax

B = 128
W = 14
P_SIZE = 16
ITERS = 3
SEGS = 16
NSEC = 16


def plant(array, rng, low, largest):
    longest = array.shape.index(max(array.shape))
    spots = []
    for shift in (0, 1):
        where = [jax.random.randint(jax.random.fold_in(rng, axis), (), 0, length) for axis, length in enumerate(array.shape)]
        where[longest] = (where[longest] + shift) % array.shape[longest]
        spots.append(tuple(where))
    return array.at[spots[0]].set(low).at[spots[1]].set(largest)


def block_levels(rng, shape, shards, smallest, largest):
    factor_of = 1.0
    for position, parts in shards:
        steps = jax.random.uniform(jax.random.fold_in(jax.random.fold_in(rng, 6), position), (parts,), jnp.float32, smallest / len(shards), largest / len(shards))
        factor_of = factor_of * jnp.repeat(jnp.exp(steps), shape[position] // parts).reshape((-1,) + (1,) * (len(shape) - 1 - position))
    return factor_of


def split_up(amount, total, limit, slope):
    weights = [(1 << 20) // math.isqrt(standing ** slope) + 1 for standing in range(2, amount + 1)]
    rest, given = total - limit - (amount - 1), [1] * (amount - 1)
    while rest > 0:
        candidates = [i for i in range(amount - 1) if given[i] < limit]
        pool, remaining = sum([weights[i] for i in candidates]), rest
        for i in candidates:
            more = min(limit - given[i], max(1, remaining * weights[i] // pool), rest)
            given[i] = given[i] + more
            rest = rest - more
    return np.array([limit] + given)


def uneven(rng, number_of, total, reach, lean):
    if number_of == 2:
        one = jax.random.randint(rng, (), max(1, total - reach), min(reach, total - 1) + 1)
        return jnp.stack([one, total - one])
    tallies = jnp.asarray(split_up(number_of, total, reach, lean), jnp.int32)
    couples = (number_of - 1) // 2
    donor, sink = tallies[1:1 + 2 * couples:2], tallies[2:2 + 2 * couples:2]
    room = jnp.minimum(donor - 1, reach - sink)
    shifted = jax.random.randint(jax.random.fold_in(rng, 1), (couples,), 0, 1 << 20) % (room + 1)
    tallies = tallies.at[1:1 + 2 * couples:2].set(donor - shifted).at[2:2 + 2 * couples:2].set(sink + shifted)
    return tallies[jax.random.permutation(jax.random.fold_in(rng, 2), number_of)]


def bell_draw(rng, shape, scale, limit, shards=(), held_as=jnp.bfloat16):
    entries = scale * jax.random.normal(rng, shape, jnp.float32)
    if shards:
        entries = entries * block_levels(rng, shape, shards, -0.22, 0.18)
    return jnp.clip(entries, -limit, limit).astype(held_as)


def setup_inputs(seed: int = 0) -> dict:
    keys = jax.random.split(jax.random.key(seed), 10)
    return {
        "left_edge": bell_draw(keys[0], (NSEC, W, B, B), B ** -0.5, 0.5, ((0, 16),), jnp.float32),
        "transfer": bell_draw(keys[1], (SEGS, NSEC, B, B), (44 * B) ** -0.5, 0.078125, ((0, 16), (1, 16)), jnp.float32),
        "completed": bell_draw(keys[2], (SEGS, NSEC, W, B, B), (4 * B) ** -0.5, 0.25, ((0, 16), (1, 16)), jnp.float32),
        "right_env": bell_draw(keys[3], (SEGS, NSEC, W, B, B), B ** -0.5, 0.5, ((0, 16), (1, 16))),
        "psi_init": bell_draw(keys[4], (SEGS, NSEC, P_SIZE, B, B), 1.0, 6.0, ((0, 16), (1, 16))),
        "mpo": bell_draw(keys[5], (W, P_SIZE, P_SIZE, W), (W * P_SIZE // 3) ** -0.5, 0.75),
        "mpo_mask": plant((jax.random.randint(keys[6], (W, W), 0, 3) < 2).astype(jnp.int32), jax.random.fold_in(keys[6], 1), 0, 1),
        "charge_shift": plant(jax.random.randint(keys[7], (NSEC, P_SIZE), -1, 2), jax.random.fold_in(keys[7], 1), -1, 1).astype(jnp.int32),
        "block_size": uneven(keys[8], NSEC, (NSEC * B * 3) // 4, B, 0).astype(jnp.int32),
    }


carry_weight = 0.8
step_size = 0.5

def to_bfloat(values):
    return lax.optimization_barrier(values.astype(jnp.bfloat16)).astype(jnp.float32)

def congruence(matrix, environ):
    inner = jnp.einsum('qwac,qcd->qwad', environ, matrix, precision=lax.Precision.HIGHEST)
    return jnp.einsum('qab,qwad->qwbd', matrix, inner, precision=lax.Precision.HIGHEST)

def reference(left_edge, transfer, completed, right_env, psi_init, mpo, mpo_mask, charge_shift, block_size):
    identity = jnp.eye(B, dtype=jnp.float32)
    environ = left_edge
    stacked = []
    for segment in range(SEGS):
        stacked.append(environ)
        environ = congruence(carry_weight * identity + transfer[segment], environ) + completed[segment]
    stacked = jnp.stack(stacked)
    sector_ids = jnp.arange(NSEC, dtype=jnp.int32)
    target = sector_ids[:, None] + charge_shift
    valid = (target >= 0) & (target < NSEC)
    clipped = jnp.clip(target, 0, NSEC - 1).astype(jnp.int32)
    row_ids = jnp.arange(B, dtype=jnp.int32)
    live_rows = row_ids[None, :] < block_size[:, None]
    right_rows = live_rows[clipped]
    mask = (valid[:, :, None, None] & live_rows[:, None, :, None] & right_rows[:, :, None, :]).astype(jnp.float32)
    allowed = (charge_shift[:, :, None] == charge_shift[:, None, :]).astype(jnp.float32)
    operator = mpo.astype(jnp.float32)[None] * mpo_mask.astype(jnp.float32)[None, :, None, None, :] * allowed[:, None, :, :, None]

    def one_segment(inputs):
        environ_c, right_c, psi_c = inputs
        chosen = right_c.astype(jnp.float32)[clipped]
        env_bf = to_bfloat(environ_c)

        def apply_ham(tensor):
            first = to_bfloat(jnp.einsum('qwae,qped->qpwad', env_bf, to_bfloat(tensor)))
            second = to_bfloat(jnp.einsum('qwpxv,qxwad->qpvad', operator, first))
            return jnp.einsum('qpvad,qpvbd->qpab', second, chosen) * mask
        tensor = mask * psi_c.astype(jnp.float32)
        rayleigh = jnp.float32(0.0)
        for step in range(ITERS):
            image = apply_ham(tensor)
            norm_sq = jnp.sum(tensor * tensor)
            intersection = jnp.sum(tensor * image)
            rayleigh = intersection / norm_sq
            updated = tensor - step_size * (image - rayleigh * tensor)
            tensor = updated / jnp.sqrt(jnp.sum(updated * updated))
        return (tensor.astype(jnp.bfloat16), rayleigh)
    psi_out, energy = lax.map(one_segment, (stacked, right_env, psi_init))
    return (psi_out, energy)
```

```python
import functools

import jax
import jax.numpy as jnp
from jax import lax
from jax.experimental import pallas as pl
from jax.experimental.pallas import tpu as pltpu
from jax.sharding import PartitionSpec as P

ITERS = 3
CARRY = 0.8
STEP = 0.5
F32 = jnp.float32
BF16 = jnp.bfloat16
VMEM_LIMIT = 56 * 2**20

SMEM_SPEC = pl.BlockSpec(memory_space=pltpu.SMEM)
VMEM_SPEC = pl.BlockSpec(memory_space=pltpu.VMEM)
ANY_SPEC = pl.BlockSpec(memory_space=pl.ANY)
PARAMS = pltpu.CompilerParams(vmem_limit_bytes=VMEM_LIMIT)

PAIRS = [(i, j) for j in range(ITERS + 1) for i in range(j + 1)]


def pack_kernel(add_ref, transfer_ref, out_ref):
    channels, rows, _ = add_ref.shape
    slots = out_ref.shape[0]
    moved = transfer_ref[...].astype(BF16)
    for w in range(slots):
        if w < channels:
            out_ref[w, :rows, :] = add_ref[w].astype(BF16)
        else:
            out_ref[w, :rows, :] = jnp.zeros((rows, rows), BF16)
        out_ref[w, rows:, :] = moved


def scan_kernel(got_ref, left_ref, right_ref, env_ref, wide_ref, edge, tall, sem):
    segments, _, rows = got_ref.shape
    channels = left_ref.shape[0]
    mine = jnp.minimum(lax.axis_index("chain"), channels - 1)
    fetch = pltpu.make_async_copy(left_ref.at[mine], edge, sem)
    fetch.start()
    slots = tall.shape[0] // rows
    for v in range(slots):
        if v < channels:
            tall[pl.ds(v, rows, stride=slots), :] = right_ref[v].astype(F32).T
        else:
            tall[pl.ds(v, rows, stride=slots), :] = jnp.zeros((rows, rows), F32)
    for n in range(slots):
        wide_ref[:, n * rows : (n + 1) * rows] = tall[n * rows : (n + 1) * rows, :].T.astype(BF16)
    fetch.wait()
    env = edge[...].T
    env_ref[0] = env.astype(BF16)
    for c in range(segments - 1):
        moved = got_ref[c, rows:, :]
        half = CARRY * env + jnp.dot(env.astype(BF16), moved, preferred_element_type=F32)
        env = (
            CARRY * half
            + jnp.dot(moved.T, half.astype(BF16), preferred_element_type=F32)
            + got_ref[c, :rows, :].astype(F32).T
        )
        env_ref[c + 1] = env.astype(BF16)


def slot_limit(q, shift, size_ref):
    sectors = size_ref.shape[0]
    target = q + shift
    valid = jnp.logical_and(target >= 0, target < sectors)
    return jnp.where(valid, size_ref[jnp.clip(target, 0, sectors - 1)], 0)


def ham_kernel(
    shift_ref, size_ref, env_ref, below_ref, own_ref, above_ref, psi_ref, mpo_ref, chan_ref,
    stats_ref, image_ref,
    vecs, unit, left, right, mix, first, second,
):
    q = lax.axis_index("sector")
    channels, states = mpo_ref.shape[:2]
    rows = psi_ref.shape[-1]
    deep = channels * states
    slots = mix.shape[0] // states
    state_of = lax.broadcasted_iota(jnp.int32, (1, deep), 1) % states
    shift_of = jnp.zeros((1, deep), jnp.int32)
    for p2 in range(states):
        shift_of = jnp.where(state_of == p2, shift_ref[0, p2], shift_of)
    spread = (
        lax.broadcasted_iota(jnp.int32, (channels, deep), 1) // states
        == lax.broadcasted_iota(jnp.int32, (channels, deep), 0)
    ).astype(F32)
    kept = lax.dot_general(
        chan_ref[...].astype(F32), spread, (((0,), (0,)), ((), ())), preferred_element_type=F32
    )
    kept = jnp.concatenate([kept, jnp.zeros((slots - channels, deep), F32)], axis=0)
    pick = (
        lax.broadcasted_iota(jnp.int32, (slots, channels), 0)
        == lax.broadcasted_iota(jnp.int32, (slots, channels), 1)
    ).astype(BF16)
    for p in range(states):
        block = jnp.concatenate([mpo_ref[w, p] for w in range(channels)], axis=0)
        turned = lax.dot_general(
            pick, block, (((1,), (1,)), ((), ())), preferred_element_type=F32
        )
        same = (shift_of == shift_ref[0, p]).astype(F32)
        mix[p * slots : (p + 1) * slots, :] = (turned * kept * same).astype(BF16)
    for w in range(channels):
        left[:, w * rows : (w + 1) * rows] = env_ref[w]
    right[0] = below_ref[...]
    right[1] = own_ref[...]
    right[2] = above_ref[...]

    row_id = lax.broadcasted_iota(jnp.int32, (rows, rows), 0)
    col_id = lax.broadcasted_iota(jnp.int32, (rows, rows), 1)
    own_size = size_ref[q]

    def masked(p, block):
        limit = slot_limit(q, shift_ref[0, p], size_ref)
        live = jnp.logical_and(row_id < limit, col_id < own_size)
        return jnp.where(live, block, 0.0)

    def inner(i, j):
        return jnp.sum(
            jnp.sum(vecs[i] * vecs[j], axis=0, keepdims=True), axis=1, keepdims=True
        )

    for p in range(states):
        vecs[0, pl.ds(p, rows, stride=states), :] = masked(p, psi_ref[p].astype(F32).T)
    gram = {(0, 0): inner(0, 0)}
    scales = []
    chunk = first.shape[0]
    for k in range(ITERS):
        size = gram[k, k]
        scale = jnp.where(size > 1e-30, lax.rsqrt(jnp.maximum(size, 1e-30)), 1.0)
        scales.append(scale)
        unit[...] = (vecs[k] * scale).astype(BF16)

        def columns(i, carry):
            start = pl.multiple_of(i * chunk * states, chunk * states)
            part = unit[pl.ds(start, chunk * states), :]
            for n in range(0, channels, 2):
                y = jnp.dot(
                    part, left[:, n * rows : (n + 2) * rows], preferred_element_type=F32
                ).astype(BF16)
                for d in range(chunk):
                    for h in range(2):
                        first[d, (n + h) * states : (n + h + 1) * states, :] = y[
                            d * states : (d + 1) * states, h * rows : (h + 1) * rows
                        ]
            for d in range(0, chunk, 2):
                pair = jnp.concatenate([first[d], first[d + 1]], axis=1)
                z = jnp.dot(mix[...], pair, preferred_element_type=F32).astype(BF16)
                for h in range(2):
                    place = pl.ds(pl.multiple_of((i * chunk + d + h) * slots, slots), slots)
                    for p in range(states):
                        second[p, place, :] = z[
                            p * slots : (p + 1) * slots, h * rows : (h + 1) * rows
                        ]
            return carry

        lax.fori_loop(0, rows // chunk, columns, 0)
        for p in range(states):
            block = jnp.dot(
                right[shift_ref[0, p] + 1], second[p], preferred_element_type=F32
            )
            block = masked(p, block)
            vecs[k + 1, pl.ds(p, rows, stride=states), :] = block
            image_ref[k, p] = block.T
        for j in range(k + 2):
            gram[j, k + 1] = inner(j, k + 1)
    entries = [jnp.broadcast_to(gram[pair], (1, rows)) for pair in PAIRS]
    entries += [jnp.broadcast_to(scale, (1, rows)) for scale in scales]
    entries.append(jnp.zeros((stats_ref.shape[1] - len(entries), rows), F32))
    stats = jnp.concatenate(entries, axis=0)
    for s in range(stats_ref.shape[0]):
        stats_ref[s] = stats


def final_kernel(shift_ref, size_ref, stats_ref, psi_ref, image_ref, out_ref, energy_ref):
    q = lax.axis_index("sector")
    sectors, _, rows = stats_ref.shape
    states = psi_ref.shape[0]
    gram = {}
    for n, (i, j) in enumerate(PAIRS):
        gram[i, j] = gram[j, i] = stats_ref[:, n, :]
    scales = [stats_ref[:, len(PAIRS) + j, :] for j in range(ITERS)]

    def product(a, b):
        total = None
        for i, x in enumerate(a):
            for j, y in enumerate(b):
                if x is not None and y is not None:
                    term = x * y * gram[i, j]
                    total = term if total is None else total + term
        return jnp.sum(total, axis=0, keepdims=True)

    coefs = [jnp.ones((sectors, rows), F32)]
    rayleigh = None
    for _ in range(ITERS):
        image = [None] + [c / s for c, s in zip(coefs, scales)]
        rayleigh = product(coefs, image) / product(coefs, coefs)
        updated = []
        for j in range(len(coefs) + 1):
            value = 0.0
            if j < len(coefs):
                value = (1.0 + STEP * rayleigh) * coefs[j]
            if image[j] is not None:
                value = value - STEP * image[j]
            updated.append(value)
        norm = lax.rsqrt(product(updated, updated))
        coefs = [c * norm for c in updated]
    energy_ref[0] = rayleigh[0, 0]
    sector_id = lax.broadcasted_iota(jnp.int32, (sectors, rows), 0)
    own = [jnp.sum(jnp.where(sector_id == q, c, 0.0), axis=0, keepdims=True) for c in coefs]
    row_id = lax.broadcasted_iota(jnp.int32, (rows, rows), 0)
    col_id = lax.broadcasted_iota(jnp.int32, (rows, rows), 1)
    own_size = size_ref[q]
    for p in range(states):
        limit = slot_limit(q, shift_ref[0, p], size_ref)
        live = jnp.logical_and(col_id < limit, row_id < own_size)
        total = own[0] * jnp.where(live, psi_ref[p].astype(F32), 0.0)
        for k in range(ITERS):
            total = total + own[k + 1] * image_ref[k, p]
        out_ref[p] = total.astype(BF16)


def body(
    left_edge, transfer, completed, right_env, psi_init, mpo, mpo_mask, charge_shift, block_size
):
    channels, rows = left_edge.shape[1:3]
    segments, sectors = lax.axis_size("chain"), lax.axis_size("sector")
    states = psi_init.shape[2]
    slots = 16
    payload = pl.pallas_call(
        pack_kernel,
        out_shape=jax.ShapeDtypeStruct((segments, 2 * rows, rows), BF16),
        in_specs=[VMEM_SPEC] * 2,
        out_specs=VMEM_SPEC,
        compiler_params=PARAMS,
    )(completed[0, 0], transfer[0, 0])
    got = lax.all_to_all(payload, "chain", 0, 0, tiled=True)
    env_out, wide = pl.pallas_call(
        scan_kernel,
        out_shape=(
            jax.ShapeDtypeStruct((segments, rows, rows), BF16),
            jax.ShapeDtypeStruct((rows, rows * slots), BF16),
        ),
        in_specs=[VMEM_SPEC, ANY_SPEC, VMEM_SPEC],
        out_specs=(VMEM_SPEC, VMEM_SPEC),
        scratch_shapes=[
            pltpu.VMEM((rows, rows), F32),
            pltpu.VMEM((rows * slots, rows), F32),
            pltpu.SemaphoreType.DMA,
        ],
        compiler_params=PARAMS,
    )(got, left_edge[0], right_env[0, 0])
    below = lax.ppermute(wide, "sector", [(i, i + 1) for i in range(sectors - 1)])
    above = lax.ppermute(wide, "sector", [(i + 1, i) for i in range(sectors - 1)])
    env = lax.all_to_all(env_out, "chain", 0, 0, tiled=True)
    chunk = 16
    stats, image = pl.pallas_call(
        ham_kernel,
        out_shape=(
            jax.ShapeDtypeStruct((sectors, 16, rows), F32),
            jax.ShapeDtypeStruct((ITERS, states, rows, rows), F32),
        ),
        in_specs=[SMEM_SPEC] * 2 + [VMEM_SPEC] * 7,
        out_specs=(VMEM_SPEC, VMEM_SPEC),
        scratch_shapes=[
            pltpu.VMEM((ITERS + 1, rows * states, rows), F32),
            pltpu.VMEM((rows * states, rows), BF16),
            pltpu.VMEM((rows, channels * rows), BF16),
            pltpu.VMEM((3, rows, rows * slots), BF16),
            pltpu.VMEM((states * slots, channels * states), BF16),
            pltpu.VMEM((chunk, channels * states, rows), BF16),
            pltpu.VMEM((states, rows * slots, rows), BF16),
        ],
        compiler_params=PARAMS,
    )(charge_shift, block_size, env, below, wide, above, psi_init[0, 0], mpo, mpo_mask)
    stats = lax.all_to_all(stats, "sector", 0, 0, tiled=True)
    out, energy = pl.pallas_call(
        final_kernel,
        out_shape=(
            jax.ShapeDtypeStruct((states, rows, rows), BF16),
            jax.ShapeDtypeStruct((1,), F32),
        ),
        in_specs=[SMEM_SPEC] * 2 + [VMEM_SPEC] * 3,
        out_specs=(VMEM_SPEC, SMEM_SPEC),
        compiler_params=PARAMS,
    )(charge_shift, block_size, stats, psi_init[0, 0], image)
    return out[None, None], energy


def solution(mesh):
    placed = (
        P("sector", None, None, None),
        P("chain", "sector", None, None),
        P("chain", "sector", None, None, None),
        P("chain", "sector", None, None, None),
        P("chain", "sector", None, None, None),
        P(),
        P(),
        P("sector", None),
        P(),
    )
    return jax.shard_map(
        body,
        mesh=mesh,
        in_specs=placed,
        out_specs=(P("chain", "sector", None, None, None), P("chain")),
        check_vma=False,
    )
```

```python
import functools

import jax
import jax.numpy as jnp
from jax import lax
from jax.experimental import pallas as pl
from jax.experimental.pallas import tpu as pltpu
from jax.sharding import PartitionSpec as P

ITERS = 3
CARRY = 0.8
STEP = 0.5
F32 = jnp.float32
BF16 = jnp.bfloat16
VMEM_LIMIT = 63 * 2**20

SMEM_SPEC = pl.BlockSpec(memory_space=pltpu.SMEM)
VMEM_SPEC = pl.BlockSpec(memory_space=pltpu.VMEM)
HBM_SPEC = pl.BlockSpec(memory_space=pltpu.HBM)

PAIRS = [(i, j) for j in range(ITERS + 1) for i in range(j + 1)]


def pack_kernel(add_ref, transfer_ref, out_ref, adds, moved, block, in_sems, out_sems):
    channels, rows, _ = add_ref.shape
    slots, group = out_ref.shape[0], channels // 7
    fetch = pltpu.make_async_copy(transfer_ref, moved, in_sems.at[7])
    fetch.start()
    fetches, stores = [], []
    for n in range(7):
        part = pl.ds(n * group, group)
        fetches.append(pltpu.make_async_copy(add_ref.at[part], adds.at[part], in_sems.at[n]))
        fetches[n].start()
    fetch.wait()
    for w in range(slots):
        block[w, rows:, :] = moved[...].astype(BF16)
    for w in range(channels, slots):
        block[w, :rows, :] = jnp.zeros((rows, rows), BF16)
    part = pl.ds(channels, slots - channels)
    stores.append(pltpu.make_async_copy(block.at[part], out_ref.at[part], out_sems.at[7]))
    stores[0].start()
    for n in range(7):
        fetches[n].wait()
        for w in range(n * group, (n + 1) * group):
            block[w, :rows, :] = adds[w].astype(BF16)
        part = pl.ds(n * group, group)
        stores.append(pltpu.make_async_copy(block.at[part], out_ref.at[part], out_sems.at[n]))
        stores[-1].start()
    for store in stores:
        store.wait()


def congruence(env, scale, rest, add):
    rest = rest.astype(BF16)
    half = scale * env + jnp.dot(env.astype(BF16), rest, preferred_element_type=F32)
    moved = scale * half + jnp.dot(rest.T, half.astype(BF16), preferred_element_type=F32)
    return moved + add


def scan_kernel(got_hbm, left_hbm, env_ref, edge, got_ref, sem, got_sems):
    segments, _, rows = got_ref.shape
    channels = left_hbm.shape[0]
    mine = jnp.minimum(lax.axis_index("chain"), channels - 1)
    fetch = pltpu.make_async_copy(left_hbm.at[mine], edge, sem)
    fetch.start()
    width = 4
    groups = segments // width
    fetches = []
    for n in range(groups):
        part = pl.ds(n * width, width)
        fetches.append(pltpu.make_async_copy(got_hbm.at[part], got_ref.at[part], got_sems.at[n]))
        fetches[n].start()
    fetch.wait()
    for n in range(groups):
        fetches[n].wait()

    def step(c):
        return got_ref[c, rows:, :], got_ref[c, :rows, :].astype(F32)

    current = [edge[...]] + [None] * (groups - 1)
    begun = [[] for _ in range(groups)]
    factors = [[] for _ in range(groups)]
    env_ref[0] = edge[...].astype(BF16)
    for j in range(width):
        for g in range(groups):
            c = g * width + j
            if c == segments - 1:
                continue
            rest, add = step(c)
            if g == 0:
                current[0] = congruence(current[0], CARRY, rest, add)
                env_ref[c + 1] = current[0].astype(BF16)
            elif j == 0:
                begun[g].append(add)
                factors[g].append((CARRY, rest))
            else:
                begun[g].append(congruence(begun[g][-1], CARRY, rest, add))
                scale, other = factors[g][-1]
                product = (
                    CARRY * other.astype(F32)
                    + scale * rest.astype(F32)
                    + jnp.dot(other.astype(BF16), rest, preferred_element_type=F32)
                )
                factors[g].append((scale * CARRY, product))
    env = current[0]
    for g in range(1, groups):
        first = env
        for j in reversed(range(len(begun[g]))):
            block = congruence(first, *factors[g][j], begun[g][j])
            env_ref[g * width + j + 1] = block.astype(BF16)
            if j == width - 1:
                env = block


def slot_limit(q, shift, size_ref):
    sectors = size_ref.shape[0]
    target = q + shift
    valid = jnp.logical_and(target >= 0, target < sectors)
    return jnp.where(valid, size_ref[jnp.clip(target, 0, sectors - 1)], 0)


def fill_operator(mix, shift_ref, mpo_ref, chan_ref, slots, by_v):
    channels, _, states, _ = mpo_ref.shape
    deep = channels * states

    def ids(shape, dim):
        return lax.broadcasted_iota(jnp.int32, shape, dim)

    total = jnp.zeros((deep, deep), F32)
    for c in range(channels):
        tiles = [mpo_ref[c, o] if by_v else mpo_ref[o, c] for o in range(channels)]
        place = (ids((states, deep), 1) == ids((states, deep), 0) + c * states).astype(BF16)
        total = total + jnp.dot(
            jnp.concatenate(tiles, axis=0), place, preferred_element_type=F32
        )
    row, col = ids((states * slots, deep), 0), ids((states * slots, deep), 1)
    order = (col == (row % slots) * states + row // slots).astype(BF16)
    total = jnp.dot(order, total.astype(BF16), preferred_element_type=F32)
    spread = (ids((channels, deep), 1) // states == ids((channels, deep), 0)).astype(F32)
    kept = lax.dot_general(
        chan_ref[...].astype(F32), spread, (((0 if by_v else 1,), (0,)), ((), ())),
        preferred_element_type=F32,
    )
    kept = jnp.concatenate([kept, jnp.zeros((slots - channels, deep), F32)], axis=0)
    state_of = ids((1, deep), 1) % states
    shift_of = jnp.zeros((1, deep), jnp.int32)
    for p in range(states):
        shift_of = jnp.where(state_of == p, shift_ref[0, p], shift_of)
    for p in range(states):
        same = (shift_of == shift_ref[0, p]).astype(F32)
        part = slice(p * slots, (p + 1) * slots)
        mix[part, :] = (total[part, :] * kept * same).astype(BF16)


def pair_up(shift_ref, pair_ref, open_ref):
    states = shift_ref.shape[1]
    for s in range(3):
        open_ref[s] = -1
    count = jnp.int32(0)
    for p in range(states):
        s = shift_ref[0, p] + 1
        waiting = open_ref[s]
        ready = waiting >= 0
        pair_ref[0, count] = jnp.where(ready, waiting, p)
        pair_ref[1, count] = p
        count = count + ready.astype(jnp.int32)
        open_ref[s] = jnp.where(ready, -1, p)
    for s in range(3):
        waiting = open_ref[s]
        pair_ref[0, count] = jnp.maximum(waiting, 0)
        pair_ref[1, count] = jnp.maximum(waiting, 0)
        count = count + (waiting >= 0).astype(jnp.int32)
    pair_ref[2, 0] = count


def block_mask(shift_ref, size_ref, rows, turned):
    q = lax.axis_index("sector")
    row_id = lax.broadcasted_iota(jnp.int32, (rows, rows), 0)
    col_id = lax.broadcasted_iota(jnp.int32, (rows, rows), 1)
    left_id, right_id = (col_id, row_id) if turned else (row_id, col_id)
    own_size = size_ref[q]

    def live(p):
        limit = slot_limit(q, shift_ref[0, p], size_ref)
        return jnp.logical_and(right_id < limit, left_id < own_size)

    return live


def prepare_kernel(
    shift_ref, size_ref, below_ref, own_ref, above_ref, psi_ref, mpo_ref, chan_ref,
    wide_ref, mix_ref, start_ref, pair_ref,
    tall, flat, open_ref,
):
    channels, rows, _ = own_ref.shape
    states = psi_ref.shape[0]
    slots = wide_ref.shape[2] // rows
    pair_up(shift_ref, pair_ref, open_ref)
    fill_operator(mix_ref, shift_ref, mpo_ref, chan_ref, slots, True)
    live = block_mask(shift_ref, size_ref, rows, False)
    for p in range(states):
        block = jnp.where(live(p), psi_ref[p].astype(F32), 0.0)
        flat[pl.ds(p, rows, stride=states), :] = block.T
    start_ref[...] = flat[...].astype(BF16)
    for s, source in enumerate((below_ref, own_ref, above_ref)):
        for v in range(slots):
            place = pl.ds(v, rows, stride=slots)
            if v < channels:
                tall[s, place, :] = source[v].astype(F32).T
            else:
                tall[s, place, :] = jnp.zeros((rows, rows), F32)
        for n in range(slots):
            wide_ref[s, :, n * rows : (n + 1) * rows] = tall[
                s, n * rows : (n + 1) * rows, :
            ].T.astype(BF16)


def ham_kernel(
    shift_ref, size_ref, pair_ref, env_ref, mix_ref, start_ref, psi_hbm, right_hbm,
    stats_ref, image_hbm,
    sums, vecs, unit, left, first, second, psi_ref, right_ref, image_ref, in_sems, image_sems,
):
    states, rows, _ = psi_ref.shape
    channels = mix_ref.shape[1] // states
    slots = mix_ref.shape[0] // states
    pairs = states // 2
    fetches = [
        pltpu.make_async_copy(psi_hbm, psi_ref, in_sems.at[0]),
        pltpu.make_async_copy(right_hbm, right_ref, in_sems.at[1]),
    ]
    for fetch in fetches:
        fetch.start()
    stores = []
    for w in range(channels):
        left[:, w * rows : (w + 1) * rows] = env_ref[w].T
    live = block_mask(shift_ref, size_ref, rows, True)

    def total(x):
        return jnp.sum(jnp.sum(x, axis=0, keepdims=True), axis=1, keepdims=True)

    begin = start_ref[...].astype(F32)
    gram = {(0, 0): total(begin * begin)}
    scales = [jnp.ones((1, 1), F32)]
    chunk = first.shape[0]
    for k in range(ITERS):
        if k:
            size = gram[k, k]
            scale = jnp.where(size > 1e-30, lax.rsqrt(jnp.maximum(size, 1e-30)), 1.0)
            scales.append(scale)
            unit[...] = (vecs[...] * scale).astype(BF16)
        source = unit if k else start_ref

        def columns(i, carry):
            start = pl.multiple_of(i * chunk * states, chunk * states)
            part = source[pl.ds(start, chunk * states), :]
            for n in range(0, channels, 2):
                y = jnp.dot(
                    part, left[:, n * rows : (n + 2) * rows], preferred_element_type=F32
                ).astype(BF16)
                for d in range(chunk):
                    for h in range(2):
                        first[d, (n + h) * states : (n + h + 1) * states, :] = y[
                            d * states : (d + 1) * states, h * rows : (h + 1) * rows
                        ]
            for d in range(0, chunk, 2):
                pair = jnp.concatenate([first[d], first[d + 1]], axis=1)
                z = jnp.dot(mix_ref[...], pair, preferred_element_type=F32).astype(BF16)
                for h in range(2):
                    place = pl.ds(pl.multiple_of((i * chunk + d + h) * slots, slots), slots)
                    for p in range(states):
                        second[p, place, :] = z[
                            p * slots : (p + 1) * slots, h * rows : (h + 1) * rows
                        ]
            return carry

        lax.fori_loop(0, rows // chunk, columns, 0)
        if k == 0:
            for fetch in fetches:
                fetch.wait()
        sums[...] = jnp.zeros(sums.shape, F32)

        def contract(n):
            members = [pair_ref[0, n], pair_ref[1, n]]
            both = jnp.concatenate([second[p] for p in members], axis=1)
            block = jnp.dot(
                right_ref[shift_ref[0, members[0]] + 1], both, preferred_element_type=F32
            )
            counts = [1.0, jnp.where(members[0] == members[1], 0.0, 1.0)]
            for h, p in enumerate(members):
                image = jnp.where(live(p), block[:, h * rows : (h + 1) * rows], 0.0)
                if k + 1 < ITERS:
                    vecs[pl.ds(p, rows, stride=states), :] = image
                image = image.T
                image_ref[k, p] = image.astype(BF16)
                for j in range(k + 2):
                    other = psi_ref[p] if j == 0 else image_ref[min(j, k) - 1, p]
                    other = image if j == k + 1 else other.astype(F32)
                    partial = jnp.sum((image * other).reshape(rows // 8, 8, rows), axis=0)
                    sums[j] += partial * counts[h]

        for n in range(pairs):
            contract(n)

        @pl.when(pair_ref[2, 0] > pairs)
        def _():
            contract(pairs)

        stores.append(pltpu.make_async_copy(image_ref.at[k], image_hbm.at[k], image_sems.at[k]))
        stores[k].start()
        for j in range(k + 2):
            gram[j, k + 1] = total(sums[j])
    entries = [jnp.broadcast_to(gram[pair], (1, rows)) for pair in PAIRS]
    entries += [jnp.broadcast_to(scale, (1, rows)) for scale in scales]
    entries.append(jnp.zeros((stats_ref.shape[1] - len(entries), rows), F32))
    stats = jnp.concatenate(entries, axis=0)
    for s in range(stats_ref.shape[0]):
        stats_ref[s] = stats
    for store in stores:
        store.wait()


def final_kernel(
    shift_ref, size_ref, stats_hbm, psi_hbm, image_hbm, out_hbm, energy_ref,
    stats_ref, psi_ref, image_ref, out_ref, stats_sem, in_sems, out_sems,
):
    stats_fetch = pltpu.make_async_copy(stats_hbm, stats_ref, stats_sem)
    stats_fetch.start()
    groups = in_sems.shape[0]
    fetches, stores = [], []
    for n in range(groups):
        part = pl.ds(n * psi_ref.shape[0] // groups, psi_ref.shape[0] // groups)
        fetches.append(
            pltpu.make_async_copy(image_hbm.at[:, part], image_ref.at[:, part], in_sems.at[n, 0])
        )
        fetches.append(pltpu.make_async_copy(psi_hbm.at[part], psi_ref.at[part], in_sems.at[n, 1]))
        stores.append(pltpu.make_async_copy(out_ref.at[part], out_hbm.at[part], out_sems.at[n]))
    for fetch in fetches:
        fetch.start()
    stats_fetch.wait()
    q = lax.axis_index("sector")
    sectors, _, rows = stats_ref.shape
    states = psi_ref.shape[0]
    gram = {}
    for n, (i, j) in enumerate(PAIRS):
        gram[i, j] = gram[j, i] = stats_ref[:, n, :]
    scales = [stats_ref[:, len(PAIRS) + j, :] for j in range(ITERS)]

    def product(a, b):
        total = None
        for i, x in enumerate(a):
            for j, y in enumerate(b):
                if x is not None and y is not None:
                    term = x * y * gram[i, j]
                    total = term if total is None else total + term
        return jnp.sum(total, axis=0, keepdims=True)

    coefs = [jnp.ones((sectors, rows), F32)]
    rayleigh = None
    for _ in range(ITERS):
        image = [None] + [c / s for c, s in zip(coefs, scales)]
        rayleigh = product(coefs, image) / product(coefs, coefs)
        updated = []
        for j in range(len(coefs) + 1):
            value = 0.0
            if j < len(coefs):
                value = (1.0 + STEP * rayleigh) * coefs[j]
            if image[j] is not None:
                value = value - STEP * image[j]
            updated.append(value)
        norm = lax.rsqrt(product(updated, updated))
        coefs = [c * norm for c in updated]
    energy_ref[0] = rayleigh[0, 0]
    sector_id = lax.broadcasted_iota(jnp.int32, (sectors, rows), 0)
    own = [jnp.sum(jnp.where(sector_id == q, c, 0.0), axis=0, keepdims=True) for c in coefs]
    row_id = lax.broadcasted_iota(jnp.int32, (rows, rows), 0)
    col_id = lax.broadcasted_iota(jnp.int32, (rows, rows), 1)
    own_size = size_ref[q]
    for p in range(states):
        if p % (states // groups) == 0:
            fetches[2 * (p * groups // states)].wait()
            fetches[2 * (p * groups // states) + 1].wait()
        limit = slot_limit(q, shift_ref[0, p], size_ref)
        live = jnp.logical_and(col_id < limit, row_id < own_size)
        total = own[0] * jnp.where(live, psi_ref[p].astype(F32), 0.0)
        for k in range(ITERS):
            total = total + own[k + 1] * image_ref[k, p].astype(F32)
        out_ref[p] = total.astype(BF16)
        if (p + 1) % (states // groups) == 0:
            stores[p * groups // states].start()
    for store in stores:
        store.wait()


def body(
    left_edge, transfer, completed, right_env, psi_init, mpo, mpo_mask, charge_shift, block_size
):
    channels, rows = left_edge.shape[1:3]
    segments, sectors = lax.axis_size("chain"), lax.axis_size("sector")
    states = psi_init.shape[2]
    slots = 16
    deep = channels * states
    own, psi = right_env[0, 0], psi_init[0, 0]
    operator = jnp.transpose(mpo, (0, 3, 1, 2))

    def kernel(function, out_shape, in_specs, scratch, out_specs=None, flops=0, grid=()):
        shapes = out_shape if isinstance(out_shape, tuple) else (out_shape,)
        specs = out_specs or tuple(VMEM_SPEC for _ in shapes)
        return pl.pallas_call(
            function,
            grid=grid,
            out_shape=out_shape,
            in_specs=in_specs,
            out_specs=specs if isinstance(out_shape, tuple) else specs[0],
            scratch_shapes=scratch,
            compiler_params=pltpu.CompilerParams(vmem_limit_bytes=VMEM_LIMIT),
            cost_estimate=pl.CostEstimate(
                flops=flops, bytes_accessed=4 * 2**20, transcendentals=0
            ),
        )

    def shape(*dims, dtype=BF16):
        return jax.ShapeDtypeStruct(dims, dtype)

    payload = kernel(
        pack_kernel,
        shape(segments, 2 * rows, rows),
        [HBM_SPEC] * 2,
        [
            pltpu.VMEM((channels, rows, rows), F32),
            pltpu.VMEM((rows, rows), F32),
            pltpu.VMEM((segments, 2 * rows, rows), BF16),
            pltpu.SemaphoreType.DMA((8,)),
            pltpu.SemaphoreType.DMA((8,)),
        ],
        out_specs=(HBM_SPEC,),
        flops=10**6,
    )(completed[0, 0], transfer[0, 0])
    below = lax.ppermute(own, "sector", [(i, i + 1) for i in range(sectors - 1)])
    above = lax.ppermute(own, "sector", [(i + 1, i) for i in range(sectors - 1)])
    got = lax.all_to_all(payload, "chain", 0, 0, tiled=True)
    env_out = kernel(
        scan_kernel,
        shape(segments, rows, rows),
        [HBM_SPEC] * 2,
        [
            pltpu.VMEM((rows, rows), F32),
            pltpu.VMEM((segments, 2 * rows, rows), BF16),
            pltpu.SemaphoreType.DMA,
            pltpu.SemaphoreType.DMA((4,)),
        ],
        flops=2 * 10**9,
    )(got, left_edge[0])
    env_out, early = lax.optimization_barrier((env_out, psi))
    env = lax.all_to_all(env_out, "chain", 0, 0, tiled=True)
    wide, mix, start, pairs = kernel(
        prepare_kernel,
        (
            shape(3, rows, rows * slots),
            shape(states * slots, deep),
            shape(rows * states, rows),
            shape(3, states, dtype=jnp.int32),
        ),
        [SMEM_SPEC] * 2 + [VMEM_SPEC] * 6,
        [
            pltpu.VMEM((3, rows * slots, rows), F32),
            pltpu.VMEM((rows * states, rows), F32),
            pltpu.SMEM((3,), jnp.int32),
        ],
        out_specs=(VMEM_SPEC,) * 3 + (SMEM_SPEC,),
        flops=5 * 10**9,
    )(charge_shift, block_size, below, own, above, early, operator, mpo_mask)
    chunk = 64
    stats, image = kernel(
        ham_kernel,
        (shape(sectors, 16, rows, dtype=F32), shape(ITERS, states, rows, rows)),
        [SMEM_SPEC] * 3 + [VMEM_SPEC] * 3 + [HBM_SPEC] * 2,
        [
            pltpu.VMEM((ITERS + 1, 8, rows), F32),
            pltpu.VMEM((rows * states, rows), F32),
            pltpu.VMEM((rows * states, rows), BF16),
            pltpu.VMEM((rows, channels * rows), BF16),
            pltpu.VMEM((chunk, deep, rows), BF16),
            pltpu.VMEM((states, rows * slots, rows), BF16),
            pltpu.VMEM((states, rows, rows), BF16),
            pltpu.VMEM((3, rows, rows * slots), BF16),
            pltpu.VMEM((ITERS, states, rows, rows), BF16),
            pltpu.SemaphoreType.DMA((2,)),
            pltpu.SemaphoreType.DMA((ITERS,)),
        ],
        out_specs=(VMEM_SPEC, HBM_SPEC),
        flops=10**10,
    )(charge_shift, block_size, pairs, env, mix, start, psi, wide)
    stats = lax.all_to_all(stats, "sector", 0, 0, tiled=True)
    out, energy = kernel(
        final_kernel,
        (shape(states, rows, rows), shape(1, dtype=F32)),
        [SMEM_SPEC] * 2 + [HBM_SPEC] * 3,
        [
            pltpu.VMEM(stats.shape, F32),
            pltpu.VMEM((states, rows, rows), BF16),
            pltpu.VMEM((ITERS, states, rows, rows), BF16),
            pltpu.VMEM((states, rows, rows), BF16),
            pltpu.SemaphoreType.DMA,
            pltpu.SemaphoreType.DMA((4, 2)),
            pltpu.SemaphoreType.DMA((4,)),
        ],
        out_specs=(HBM_SPEC, SMEM_SPEC),
        flops=10**7,
    )(charge_shift, block_size, stats, psi, image)
    return out[None, None], energy


def solution(mesh):
    placed = (
        P("sector", None, None, None),
        P("chain", "sector", None, None),
        P("chain", "sector", None, None, None),
        P("chain", "sector", None, None, None),
        P("chain", "sector", None, None, None),
        P(),
        P(),
        P("sector", None),
        P(),
    )
    return jax.shard_map(
        body,
        mesh=mesh,
        in_specs=placed,
        out_specs=(P("chain", "sector", None, None, None), P("chain")),
        check_vma=False,
    )
```

```python
import functools

import jax
import jax.numpy as jnp
from jax import lax
from jax.experimental import pallas as pl
from jax.experimental.pallas import tpu as pltpu
from jax.sharding import PartitionSpec as P

ITERS = 3
CARRY = 0.8
STEP = 0.5
F32 = jnp.float32
BF16 = jnp.bfloat16
VMEM_LIMIT = 63 * 2**20

SMEM_SPEC = pl.BlockSpec(memory_space=pltpu.SMEM)
VMEM_SPEC = pl.BlockSpec(memory_space=pltpu.VMEM)
HBM_SPEC = pl.BlockSpec(memory_space=pltpu.HBM)

PAIRS = [(i, j) for j in range(ITERS + 1) for i in range(j + 1)]


def pack_kernel(add_ref, transfer_ref, out_ref, adds, moved, block, in_sems, out_sems):
    channels, rows, _ = add_ref.shape
    slots, group = out_ref.shape[0], channels // 7
    fetch = pltpu.make_async_copy(transfer_ref, moved, in_sems.at[7])
    fetch.start()
    fetches, stores = [], []
    for n in range(7):
        part = pl.ds(n * group, group)
        fetches.append(pltpu.make_async_copy(add_ref.at[part], adds.at[part], in_sems.at[n]))
        fetches[n].start()
    fetch.wait()
    for w in range(slots):
        block[w, rows:, :] = moved[...].astype(BF16)
    for w in range(channels, slots):
        block[w, :rows, :] = jnp.zeros((rows, rows), BF16)
    part = pl.ds(channels, slots - channels)
    stores.append(pltpu.make_async_copy(block.at[part], out_ref.at[part], out_sems.at[7]))
    stores[0].start()
    for n in range(7):
        fetches[n].wait()
        for w in range(n * group, (n + 1) * group):
            block[w, :rows, :] = adds[w].astype(BF16)
        part = pl.ds(n * group, group)
        stores.append(pltpu.make_async_copy(block.at[part], out_ref.at[part], out_sems.at[n]))
        stores[-1].start()
    for store in stores:
        store.wait()


def congruence(env, scale, rest, add):
    rest = rest.astype(BF16)
    half = scale * env + jnp.dot(env.astype(BF16), rest, preferred_element_type=F32)
    moved = scale * half + jnp.dot(rest.T, half.astype(BF16), preferred_element_type=F32)
    return moved + add


def scan_kernel(got_hbm, left_hbm, env_ref, edge, got_ref, sem, got_sems):
    segments, _, rows = got_ref.shape
    channels = left_hbm.shape[0]
    mine = jnp.minimum(lax.axis_index("chain"), channels - 1)
    fetch = pltpu.make_async_copy(left_hbm.at[mine], edge, sem)
    fetch.start()
    width = 4
    groups = segments // width
    fetches = []
    for n in range(groups):
        part = pl.ds(n * width, width)
        fetches.append(pltpu.make_async_copy(got_hbm.at[part], got_ref.at[part], got_sems.at[n]))
        fetches[n].start()
    fetch.wait()
    for n in range(groups):
        fetches[n].wait()

    def step(c):
        return got_ref[c, rows:, :], got_ref[c, :rows, :].astype(F32)

    current = [edge[...]] + [None] * (groups - 1)
    begun = [[] for _ in range(groups)]
    factors = [[] for _ in range(groups)]
    env_ref[0] = edge[...].astype(BF16)
    for j in range(width):
        for g in range(groups):
            c = g * width + j
            if c == segments - 1:
                continue
            rest, add = step(c)
            if g == 0:
                current[0] = congruence(current[0], CARRY, rest, add)
                env_ref[c + 1] = current[0].astype(BF16)
            elif j == 0:
                begun[g].append(add)
                factors[g].append((CARRY, rest))
            else:
                begun[g].append(congruence(begun[g][-1], CARRY, rest, add))
                scale, other = factors[g][-1]
                product = (
                    CARRY * other.astype(F32)
                    + scale * rest.astype(F32)
                    + jnp.dot(other.astype(BF16), rest, preferred_element_type=F32)
                )
                factors[g].append((scale * CARRY, product))
    env = current[0]
    for g in range(1, groups):
        first = env
        for j in reversed(range(len(begun[g]))):
            block = congruence(first, *factors[g][j], begun[g][j])
            env_ref[g * width + j + 1] = block.astype(BF16)
            if j == width - 1:
                env = block


def slot_limit(q, shift, size_ref):
    sectors = size_ref.shape[0]
    target = q + shift
    valid = jnp.logical_and(target >= 0, target < sectors)
    return jnp.where(valid, size_ref[jnp.clip(target, 0, sectors - 1)], 0)


def fill_operator(mix, shift_ref, mpo_ref, chan_ref, slots, by_v):
    channels, _, states, _ = mpo_ref.shape
    deep = channels * states

    def ids(shape, dim):
        return lax.broadcasted_iota(jnp.int32, shape, dim)

    total = jnp.zeros((deep, deep), F32)
    for c in range(channels):
        tiles = [mpo_ref[c, o] if by_v else mpo_ref[o, c] for o in range(channels)]
        place = (ids((states, deep), 1) == ids((states, deep), 0) + c * states).astype(BF16)
        total = total + jnp.dot(
            jnp.concatenate(tiles, axis=0), place, preferred_element_type=F32
        )
    row, col = ids((states * slots, deep), 0), ids((states * slots, deep), 1)
    order = (col == (row % slots) * states + row // slots).astype(BF16)
    total = jnp.dot(order, total.astype(BF16), preferred_element_type=F32)
    spread = (ids((channels, deep), 1) // states == ids((channels, deep), 0)).astype(F32)
    kept = lax.dot_general(
        chan_ref[...].astype(F32), spread, (((0 if by_v else 1,), (0,)), ((), ())),
        preferred_element_type=F32,
    )
    kept = jnp.concatenate([kept, jnp.zeros((slots - channels, deep), F32)], axis=0)
    state_of = ids((1, deep), 1) % states
    shift_of = jnp.zeros((1, deep), jnp.int32)
    for p in range(states):
        shift_of = jnp.where(state_of == p, shift_ref[0, p], shift_of)
    for p in range(states):
        same = (shift_of == shift_ref[0, p]).astype(F32)
        part = slice(p * slots, (p + 1) * slots)
        mix[part, :] = (total[part, :] * kept * same).astype(BF16)


def pair_up(shift_ref, pair_ref, open_ref):
    states = shift_ref.shape[1]
    for s in range(3):
        open_ref[s] = -1
    count = jnp.int32(0)
    for p in range(states):
        s = shift_ref[0, p] + 1
        waiting = open_ref[s]
        ready = waiting >= 0
        pair_ref[0, count] = jnp.where(ready, waiting, p)
        pair_ref[1, count] = p
        count = count + ready.astype(jnp.int32)
        open_ref[s] = jnp.where(ready, -1, p)
    for s in range(3):
        waiting = open_ref[s]
        pair_ref[0, count] = jnp.maximum(waiting, 0)
        pair_ref[1, count] = jnp.maximum(waiting, 0)
        count = count + (waiting >= 0).astype(jnp.int32)
    pair_ref[2, 0] = count


def block_mask(shift_ref, size_ref, rows, turned):
    q = lax.axis_index("sector")
    row_id = lax.broadcasted_iota(jnp.int32, (rows, rows), 0)
    col_id = lax.broadcasted_iota(jnp.int32, (rows, rows), 1)
    left_id, right_id = (col_id, row_id) if turned else (row_id, col_id)
    own_size = size_ref[q]

    def live(p):
        limit = slot_limit(q, shift_ref[0, p], size_ref)
        return jnp.logical_and(right_id < limit, left_id < own_size)

    return live


def prepare_kernel(
    shift_ref, size_ref, below_ref, own_ref, above_ref, psi_ref, mpo_ref, chan_ref,
    wide_ref, mix_ref, start_ref, pair_ref,
    tall, flat, open_ref,
):
    channels, rows, _ = own_ref.shape
    states = psi_ref.shape[0]
    slots = wide_ref.shape[2] // rows
    pair_up(shift_ref, pair_ref, open_ref)
    fill_operator(mix_ref, shift_ref, mpo_ref, chan_ref, slots, True)
    live = block_mask(shift_ref, size_ref, rows, False)
    for p in range(states):
        block = jnp.where(live(p), psi_ref[p].astype(F32), 0.0)
        flat[pl.ds(p, rows, stride=states), :] = block.T
    start_ref[...] = flat[...].astype(BF16)
    for s, source in enumerate((below_ref, own_ref, above_ref)):
        for v in range(slots):
            place = pl.ds(v, rows, stride=slots)
            if v < channels:
                tall[s, place, :] = source[v].astype(F32).T
            else:
                tall[s, place, :] = jnp.zeros((rows, rows), F32)
        for n in range(slots):
            wide_ref[s, :, n * rows : (n + 1) * rows] = tall[
                s, n * rows : (n + 1) * rows, :
            ].T.astype(BF16)


def ham_kernel(
    shift_ref, size_ref, pair_ref, env_ref, mix_ref, start_ref, psi_hbm, right_hbm,
    stats_hbm, image_hbm,
    stats_ref, sums, vecs, unit, left, first, second, psi_ref, right_ref, image_ref,
    in_sems, image_sems,
):
    states, rows, _ = psi_ref.shape
    channels = mix_ref.shape[1] // states
    slots = mix_ref.shape[0] // states
    pairs = states // 2
    fetches = [
        pltpu.make_async_copy(psi_hbm, psi_ref, in_sems.at[0]),
        pltpu.make_async_copy(right_hbm, right_ref, in_sems.at[1]),
    ]
    for fetch in fetches:
        fetch.start()
    stores = []
    for w in range(channels):
        left[:, w * rows : (w + 1) * rows] = env_ref[w].T
    live = block_mask(shift_ref, size_ref, rows, True)

    def total(x):
        return jnp.sum(jnp.sum(x, axis=0, keepdims=True), axis=1, keepdims=True)

    begin = start_ref[...].astype(F32)
    gram = {(0, 0): total(begin * begin)}
    scales = [jnp.ones((1, 1), F32)]
    chunk = first.shape[0]
    for k in range(ITERS):
        if k:
            size = gram[k, k]
            scale = jnp.where(size > 1e-30, lax.rsqrt(jnp.maximum(size, 1e-30)), 1.0)
            scales.append(scale)
            unit[...] = (vecs[...] * scale).astype(BF16)
        source = unit if k else start_ref

        def columns(i, carry):
            start = pl.multiple_of(i * chunk * states, chunk * states)
            part = source[pl.ds(start, chunk * states), :]
            for n in range(0, channels, 2):
                y = jnp.dot(
                    part, left[:, n * rows : (n + 2) * rows], preferred_element_type=F32
                ).astype(BF16)
                for d in range(chunk):
                    for h in range(2):
                        first[d, (n + h) * states : (n + h + 1) * states, :] = y[
                            d * states : (d + 1) * states, h * rows : (h + 1) * rows
                        ]
            for d in range(0, chunk, 2):
                pair = jnp.concatenate([first[d], first[d + 1]], axis=1)
                z = jnp.dot(mix_ref[...], pair, preferred_element_type=F32).astype(BF16)
                for h in range(2):
                    place = pl.ds(pl.multiple_of((i * chunk + d + h) * slots, slots), slots)
                    for p in range(states):
                        second[p, place, :] = z[
                            p * slots : (p + 1) * slots, h * rows : (h + 1) * rows
                        ]
            return carry

        lax.fori_loop(0, rows // chunk, columns, 0)
        if k == 0:
            for fetch in fetches:
                fetch.wait()
        sums[...] = jnp.zeros(sums.shape, F32)

        def contract(n):
            members = [pair_ref[0, n], pair_ref[1, n]]
            both = jnp.concatenate([second[p] for p in members], axis=1)
            block = jnp.dot(
                right_ref[shift_ref[0, members[0]] + 1], both, preferred_element_type=F32
            )
            counts = [1.0, jnp.where(members[0] == members[1], 0.0, 1.0)]
            for h, p in enumerate(members):
                image = jnp.where(live(p), block[:, h * rows : (h + 1) * rows], 0.0)
                if k + 1 < ITERS:
                    vecs[pl.ds(p, rows, stride=states), :] = image
                image = image.T
                image_ref[k, p] = image.astype(BF16)
                for j in range(k + 2):
                    other = psi_ref[p] if j == 0 else image_ref[min(j, k) - 1, p]
                    other = image if j == k + 1 else other.astype(F32)
                    partial = jnp.sum((image * other).reshape(rows // 8, 8, rows), axis=0)
                    sums[j] += partial * counts[h]

        for n in range(pairs):
            contract(n)

        @pl.when(pair_ref[2, 0] > pairs)
        def _():
            contract(pairs)

        stores.append(pltpu.make_async_copy(image_ref.at[k], image_hbm.at[k], image_sems.at[k]))
        stores[k].start()
        for j in range(k + 2):
            gram[j, k + 1] = total(sums[j])
    entries = [jnp.broadcast_to(gram[pair], (1, rows)) for pair in PAIRS]
    entries += [jnp.broadcast_to(scale, (1, rows)) for scale in scales]
    entries.append(jnp.zeros((stats_ref.shape[1] - len(entries), rows), F32))
    stats = jnp.concatenate(entries, axis=0)
    for s in range(stats_ref.shape[0]):
        stats_ref[s] = stats
    stores.append(pltpu.make_async_copy(stats_ref, stats_hbm, image_sems.at[ITERS]))
    stores[ITERS].start()
    for store in stores:
        store.wait()


def final_kernel(shift_ref, size_ref, stats_ref, psi_ref, image_ref, out_ref, energy_ref):
    q = lax.axis_index("sector")
    sectors, _, rows = stats_ref.shape
    states = psi_ref.shape[0]
    gram = {}
    for n, (i, j) in enumerate(PAIRS):
        gram[i, j] = gram[j, i] = stats_ref[:, n, :]
    scales = [stats_ref[:, len(PAIRS) + j, :] for j in range(ITERS)]

    def product(a, b):
        total = None
        for i, x in enumerate(a):
            for j, y in enumerate(b):
                if x is not None and y is not None:
                    term = x * y * gram[i, j]
                    total = term if total is None else total + term
        return jnp.sum(total, axis=0, keepdims=True)

    coefs = [jnp.ones((sectors, rows), F32)]
    rayleigh = None
    for _ in range(ITERS):
        image = [None] + [c / s for c, s in zip(coefs, scales)]
        rayleigh = product(coefs, image) / product(coefs, coefs)
        updated = []
        for j in range(len(coefs) + 1):
            value = 0.0
            if j < len(coefs):
                value = (1.0 + STEP * rayleigh) * coefs[j]
            if image[j] is not None:
                value = value - STEP * image[j]
            updated.append(value)
        norm = lax.rsqrt(product(updated, updated))
        coefs = [c * norm for c in updated]
    energy_ref[0] = rayleigh[0, 0]
    sector_id = lax.broadcasted_iota(jnp.int32, (sectors, rows), 0)
    own = [jnp.sum(jnp.where(sector_id == q, c, 0.0), axis=0, keepdims=True) for c in coefs]
    row_id = lax.broadcasted_iota(jnp.int32, (rows, rows), 0)
    col_id = lax.broadcasted_iota(jnp.int32, (rows, rows), 1)
    own_size = size_ref[q]
    for p in range(states):
        limit = slot_limit(q, shift_ref[0, p], size_ref)
        live = jnp.logical_and(col_id < limit, row_id < own_size)
        total = own[0] * jnp.where(live, psi_ref[p].astype(F32), 0.0)
        for k in range(ITERS):
            total = total + own[k + 1] * image_ref[k, p].astype(F32)
        out_ref[p] = total.astype(BF16)


def body(
    left_edge, transfer, completed, right_env, psi_init, mpo, mpo_mask, charge_shift, block_size
):
    channels, rows = left_edge.shape[1:3]
    segments, sectors = lax.axis_size("chain"), lax.axis_size("sector")
    states = psi_init.shape[2]
    slots = 16
    deep = channels * states
    own, psi = right_env[0, 0], psi_init[0, 0]
    operator = jnp.transpose(mpo, (0, 3, 1, 2))

    def kernel(function, out_shape, in_specs, scratch, out_specs=None, flops=0, grid=()):
        shapes = out_shape if isinstance(out_shape, tuple) else (out_shape,)
        specs = out_specs or tuple(VMEM_SPEC for _ in shapes)
        return pl.pallas_call(
            function,
            grid=grid,
            out_shape=out_shape,
            in_specs=in_specs,
            out_specs=specs if isinstance(out_shape, tuple) else specs[0],
            scratch_shapes=scratch,
            compiler_params=pltpu.CompilerParams(vmem_limit_bytes=VMEM_LIMIT),
            cost_estimate=pl.CostEstimate(
                flops=flops, bytes_accessed=4 * 2**20, transcendentals=0
            ),
        )

    def shape(*dims, dtype=BF16):
        return jax.ShapeDtypeStruct(dims, dtype)

    payload = kernel(
        pack_kernel,
        shape(segments, 2 * rows, rows),
        [HBM_SPEC] * 2,
        [
            pltpu.VMEM((channels, rows, rows), F32),
            pltpu.VMEM((rows, rows), F32),
            pltpu.VMEM((segments, 2 * rows, rows), BF16),
            pltpu.SemaphoreType.DMA((8,)),
            pltpu.SemaphoreType.DMA((8,)),
        ],
        out_specs=(HBM_SPEC,),
        flops=10**6,
    )(completed[0, 0], transfer[0, 0])
    below = lax.ppermute(own, "sector", [(i, i + 1) for i in range(sectors - 1)])
    above = lax.ppermute(own, "sector", [(i + 1, i) for i in range(sectors - 1)])
    got = lax.all_to_all(payload, "chain", 0, 0, tiled=True)
    env_out = kernel(
        scan_kernel,
        shape(segments, rows, rows),
        [HBM_SPEC] * 2,
        [
            pltpu.VMEM((rows, rows), F32),
            pltpu.VMEM((segments, 2 * rows, rows), BF16),
            pltpu.SemaphoreType.DMA,
            pltpu.SemaphoreType.DMA((4,)),
        ],
        flops=2 * 10**9,
    )(got, left_edge[0])
    env_out, early = lax.optimization_barrier((env_out, psi))
    env = lax.all_to_all(env_out, "chain", 0, 0, tiled=True)
    wide, mix, start, pairs = kernel(
        prepare_kernel,
        (
            shape(3, rows, rows * slots),
            shape(states * slots, deep),
            shape(rows * states, rows),
            shape(3, states, dtype=jnp.int32),
        ),
        [SMEM_SPEC] * 2 + [VMEM_SPEC] * 6,
        [
            pltpu.VMEM((3, rows * slots, rows), F32),
            pltpu.VMEM((rows * states, rows), F32),
            pltpu.SMEM((3,), jnp.int32),
        ],
        out_specs=(VMEM_SPEC,) * 3 + (SMEM_SPEC,),
        flops=5 * 10**9,
    )(charge_shift, block_size, below, own, above, early, operator, mpo_mask)
    chunk = 64
    stats, image = kernel(
        ham_kernel,
        (shape(sectors, 16, rows, dtype=F32), shape(ITERS, states, rows, rows)),
        [SMEM_SPEC] * 3 + [VMEM_SPEC] * 3 + [HBM_SPEC] * 2,
        [
            pltpu.VMEM((sectors, 16, rows), F32),
            pltpu.VMEM((ITERS + 1, 8, rows), F32),
            pltpu.VMEM((rows * states, rows), F32),
            pltpu.VMEM((rows * states, rows), BF16),
            pltpu.VMEM((rows, channels * rows), BF16),
            pltpu.VMEM((chunk, deep, rows), BF16),
            pltpu.VMEM((states, rows * slots, rows), BF16),
            pltpu.VMEM((states, rows, rows), BF16),
            pltpu.VMEM((3, rows, rows * slots), BF16),
            pltpu.VMEM((ITERS, states, rows, rows), BF16),
            pltpu.SemaphoreType.DMA((2,)),
            pltpu.SemaphoreType.DMA((ITERS + 1,)),
        ],
        out_specs=(HBM_SPEC, HBM_SPEC),
        flops=10**10,
    )(charge_shift, block_size, pairs, env, mix, start, psi, wide)
    stats = lax.all_to_all(stats, "sector", 0, 0, tiled=True)
    out, energy = kernel(
        final_kernel,
        (shape(states, rows, rows), shape(1, dtype=F32)),
        [SMEM_SPEC] * 2 + [VMEM_SPEC] * 3,
        [],
        out_specs=(VMEM_SPEC, SMEM_SPEC),
        flops=10**7,
    )(charge_shift, block_size, stats, psi, image)
    return out[None, None], energy


def solution(mesh):
    placed = (
        P("sector", None, None, None),
        P("chain", "sector", None, None),
        P("chain", "sector", None, None, None),
        P("chain", "sector", None, None, None),
        P("chain", "sector", None, None, None),
        P(),
        P(),
        P("sector", None),
        P(),
    )
    return jax.shard_map(
        body,
        mesh=mesh,
        in_specs=placed,
        out_specs=(P("chain", "sector", None, None, None), P("chain")),
        check_vma=False,
    )
```

```python
import functools

import jax
import jax.numpy as jnp
from jax import lax
from jax.experimental import pallas as pl
from jax.experimental.pallas import tpu as pltpu
from jax.sharding import PartitionSpec as P

ITERS = 3
CARRY = 0.8
STEP = 0.5
F32 = jnp.float32
BF16 = jnp.bfloat16
SMEM_SPEC = pl.BlockSpec(memory_space=pltpu.SMEM)
VMEM_SPEC = pl.BlockSpec(memory_space=pltpu.VMEM)
HBM_SPEC = pl.BlockSpec(memory_space=pltpu.HBM)

PAIRS = [(i, j) for j in range(ITERS + 1) for i in range(j + 1)]


def pack_kernel(add_ref, transfer_ref, out_ref, adds, moved, block, in_sems, out_sems):
    channels, rows, _ = add_ref.shape
    slots, group = out_ref.shape[0], channels // 7
    fetch = pltpu.make_async_copy(transfer_ref, moved, in_sems.at[7])
    fetch.start()
    fetches, stores = [], []
    for n in range(7):
        part = pl.ds(n * group, group)
        fetches.append(pltpu.make_async_copy(add_ref.at[part], adds.at[part], in_sems.at[n]))
        fetches[n].start()
    fetch.wait()
    for w in range(slots):
        block[w, rows:, :] = moved[...].astype(BF16)
    for w in range(channels, slots):
        block[w, :rows, :] = jnp.zeros((rows, rows), BF16)
    part = pl.ds(channels, slots - channels)
    stores.append(pltpu.make_async_copy(block.at[part], out_ref.at[part], out_sems.at[7]))
    stores[0].start()
    for n in range(7):
        fetches[n].wait()
        for w in range(n * group, (n + 1) * group):
            block[w, :rows, :] = adds[w].astype(BF16)
        part = pl.ds(n * group, group)
        stores.append(pltpu.make_async_copy(block.at[part], out_ref.at[part], out_sems.at[n]))
        stores[-1].start()
    for store in stores:
        store.wait()


def congruence(env, scale, rest, add):
    rest = rest.astype(BF16)
    half = scale * env + jnp.dot(env.astype(BF16), rest, preferred_element_type=F32)
    moved = scale * half + jnp.dot(rest.T, half.astype(BF16), preferred_element_type=F32)
    return moved + add


def scan_kernel(got_hbm, left_hbm, env_ref, edge, got_ref, sem, got_sems):
    segments, _, rows = got_ref.shape
    channels = left_hbm.shape[0]
    mine = jnp.minimum(lax.axis_index("chain"), channels - 1)
    fetch = pltpu.make_async_copy(left_hbm.at[mine], edge, sem)
    fetch.start()
    width = 4
    groups = segments // width
    fetches = []
    for n in range(groups):
        part = pl.ds(n * width, width)
        fetches.append(pltpu.make_async_copy(got_hbm.at[part], got_ref.at[part], got_sems.at[n]))
        fetches[n].start()
    fetch.wait()
    for n in range(groups):
        fetches[n].wait()

    def step(c):
        return got_ref[c, rows:, :], got_ref[c, :rows, :].astype(F32)

    current = [edge[...]] + [None] * (groups - 1)
    begun = [[] for _ in range(groups)]
    factors = [[] for _ in range(groups)]
    env_ref[0] = edge[...].astype(BF16)
    for j in range(width):
        for g in range(groups):
            c = g * width + j
            if c == segments - 1:
                continue
            rest, add = step(c)
            if g == 0:
                current[0] = congruence(current[0], CARRY, rest, add)
                env_ref[c + 1] = current[0].astype(BF16)
            elif j == 0:
                begun[g].append(add)
                factors[g].append((CARRY, rest))
            else:
                begun[g].append(congruence(begun[g][-1], CARRY, rest, add))
                scale, other = factors[g][-1]
                product = (
                    CARRY * other.astype(F32)
                    + scale * rest.astype(F32)
                    + jnp.dot(other.astype(BF16), rest, preferred_element_type=F32)
                )
                factors[g].append((scale * CARRY, product))
    env = current[0]
    for g in range(1, groups):
        first = env
        for j in reversed(range(len(begun[g]))):
            block = congruence(first, *factors[g][j], begun[g][j])
            env_ref[g * width + j + 1] = block.astype(BF16)
            if j == width - 1:
                env = block


def slot_limit(q, shift, size_ref):
    sectors = size_ref.shape[0]
    target = q + shift
    valid = jnp.logical_and(target >= 0, target < sectors)
    return jnp.where(valid, size_ref[jnp.clip(target, 0, sectors - 1)], 0)


def fill_operator(mix, shift_ref, mpo_ref, chan_ref, slots, by_v):
    channels, _, states, _ = mpo_ref.shape
    deep = channels * states

    def ids(shape, dim):
        return lax.broadcasted_iota(jnp.int32, shape, dim)

    total = jnp.zeros((deep, deep), F32)
    for c in range(channels):
        tiles = [mpo_ref[c, o] if by_v else mpo_ref[o, c] for o in range(channels)]
        place = (ids((states, deep), 1) == ids((states, deep), 0) + c * states).astype(BF16)
        total = total + jnp.dot(
            jnp.concatenate(tiles, axis=0), place, preferred_element_type=F32
        )
    row, col = ids((states * slots, deep), 0), ids((states * slots, deep), 1)
    order = (col == (row % slots) * states + row // slots).astype(BF16)
    total = jnp.dot(order, total.astype(BF16), preferred_element_type=F32)
    spread = (ids((channels, deep), 1) // states == ids((channels, deep), 0)).astype(F32)
    kept = lax.dot_general(
        chan_ref[...].astype(F32), spread, (((0 if by_v else 1,), (0,)), ((), ())),
        preferred_element_type=F32,
    )
    kept = jnp.concatenate([kept, jnp.zeros((slots - channels, deep), F32)], axis=0)
    state_of = ids((1, deep), 1) % states
    shift_of = jnp.zeros((1, deep), jnp.int32)
    for p in range(states):
        shift_of = jnp.where(state_of == p, shift_ref[0, p], shift_of)
    for p in range(states):
        same = (shift_of == shift_ref[0, p]).astype(F32)
        part = slice(p * slots, (p + 1) * slots)
        mix[part, :] = (total[part, :] * kept * same).astype(BF16)


def pair_up(shift_ref, pair_ref, open_ref):
    states = shift_ref.shape[1]
    for s in range(3):
        open_ref[s] = -1
    count = jnp.int32(0)
    for p in range(states):
        s = shift_ref[0, p] + 1
        waiting = open_ref[s]
        ready = waiting >= 0
        pair_ref[0, count] = jnp.where(ready, waiting, p)
        pair_ref[1, count] = p
        count = count + ready.astype(jnp.int32)
        open_ref[s] = jnp.where(ready, -1, p)
    for s in range(3):
        waiting = open_ref[s]
        pair_ref[0, count] = jnp.maximum(waiting, 0)
        pair_ref[1, count] = jnp.maximum(waiting, 0)
        count = count + (waiting >= 0).astype(jnp.int32)
    pair_ref[2, 0] = count


def block_mask(shift_ref, size_ref, rows, turned):
    q = lax.axis_index("sector")
    row_id = lax.broadcasted_iota(jnp.int32, (rows, rows), 0)
    col_id = lax.broadcasted_iota(jnp.int32, (rows, rows), 1)
    left_id, right_id = (col_id, row_id) if turned else (row_id, col_id)
    own_size = size_ref[q]

    def live(p):
        limit = slot_limit(q, shift_ref[0, p], size_ref)
        return jnp.logical_and(right_id < limit, left_id < own_size)

    return live


def prepare_kernel(
    shift_ref, size_ref, below_ref, own_ref, above_ref, psi_ref, mpo_ref, chan_ref,
    wide_ref, mix_ref, start_ref, pair_ref,
    tall, flat, open_ref,
):
    channels, rows, _ = own_ref.shape
    states = psi_ref.shape[0]
    slots = wide_ref.shape[2] // rows
    pair_up(shift_ref, pair_ref, open_ref)
    fill_operator(mix_ref, shift_ref, mpo_ref, chan_ref, slots, True)
    live = block_mask(shift_ref, size_ref, rows, False)
    for p in range(states):
        block = jnp.where(live(p), psi_ref[p].astype(F32), 0.0)
        flat[pl.ds(p, rows, stride=states), :] = block.T
    start_ref[...] = flat[...].astype(BF16)
    for s, source in enumerate((below_ref, own_ref, above_ref)):
        for v in range(slots):
            place = pl.ds(v, rows, stride=slots)
            if v < channels:
                tall[s, place, :] = source[v].astype(F32).T
            else:
                tall[s, place, :] = jnp.zeros((rows, rows), F32)
        for n in range(slots):
            wide_ref[s, :, n * rows : (n + 1) * rows] = tall[
                s, n * rows : (n + 1) * rows, :
            ].T.astype(BF16)


def ham_kernel(
    shift_ref, size_ref, pair_ref, env_ref, mix_ref, start_ref, psi_hbm, right_hbm,
    stats_hbm, image_hbm,
    stats_ref, sums, vecs, unit, left, first, second, psi_ref, right_ref, image_ref,
    in_sems, image_sems,
):
    states, rows, _ = psi_ref.shape
    channels = mix_ref.shape[1] // states
    slots = mix_ref.shape[0] // states
    pairs = states // 2
    fetches = [
        pltpu.make_async_copy(psi_hbm, psi_ref, in_sems.at[0]),
        pltpu.make_async_copy(right_hbm, right_ref, in_sems.at[1]),
    ]
    for fetch in fetches:
        fetch.start()
    stores = []
    for w in range(channels):
        left[:, w * rows : (w + 1) * rows] = env_ref[w].T
    live = block_mask(shift_ref, size_ref, rows, True)

    def total(x):
        return jnp.sum(jnp.sum(x, axis=0, keepdims=True), axis=1, keepdims=True)

    begin = start_ref[...].astype(F32)
    gram = {(0, 0): total(begin * begin)}
    scales = [jnp.ones((1, 1), F32)]
    chunk = first.shape[0]
    for k in range(ITERS):
        if k:
            size = gram[k, k]
            scale = jnp.where(size > 1e-30, lax.rsqrt(jnp.maximum(size, 1e-30)), 1.0)
            scales.append(scale)
            unit[...] = (vecs[...] * scale).astype(BF16)
        source = unit if k else start_ref

        def columns(i, carry):
            start = pl.multiple_of(i * chunk * states, chunk * states)
            part = source[pl.ds(start, chunk * states), :]
            for n in range(0, channels, 2):
                y = jnp.dot(
                    part, left[:, n * rows : (n + 2) * rows], preferred_element_type=F32
                ).astype(BF16)
                for d in range(chunk):
                    for h in range(2):
                        first[d, (n + h) * states : (n + h + 1) * states, :] = y[
                            d * states : (d + 1) * states, h * rows : (h + 1) * rows
                        ]
            for d in range(0, chunk, 2):
                pair = jnp.concatenate([first[d], first[d + 1]], axis=1)
                z = jnp.dot(mix_ref[...], pair, preferred_element_type=F32).astype(BF16)
                for h in range(2):
                    place = pl.ds(pl.multiple_of((i * chunk + d + h) * slots, slots), slots)
                    for p in range(states):
                        second[p, place, :] = z[
                            p * slots : (p + 1) * slots, h * rows : (h + 1) * rows
                        ]
            return carry

        lax.fori_loop(0, rows // chunk, columns, 0)
        if k == 0:
            for fetch in fetches:
                fetch.wait()
        sums[...] = jnp.zeros(sums.shape, F32)

        def contract(n):
            members = [pair_ref[0, n], pair_ref[1, n]]
            both = jnp.concatenate([second[p] for p in members], axis=1)
            block = jnp.dot(
                right_ref[shift_ref[0, members[0]] + 1], both, preferred_element_type=F32
            )
            counts = [1.0, jnp.where(members[0] == members[1], 0.0, 1.0)]
            for h, p in enumerate(members):
                image = jnp.where(live(p), block[:, h * rows : (h + 1) * rows], 0.0)
                if k + 1 < ITERS:
                    vecs[pl.ds(p, rows, stride=states), :] = image
                image = image.T
                image_ref[k, p] = image.astype(BF16)
                for j in range(k + 2):
                    other = psi_ref[p] if j == 0 else image_ref[min(j, k) - 1, p]
                    other = image if j == k + 1 else other.astype(F32)
                    partial = jnp.sum((image * other).reshape(rows // 8, 8, rows), axis=0)
                    sums[j] += partial * counts[h]

        for n in range(pairs):
            contract(n)

        @pl.when(pair_ref[2, 0] > pairs)
        def _():
            contract(pairs)

        stores.append(pltpu.make_async_copy(image_ref.at[k], image_hbm.at[k], image_sems.at[k]))
        stores[k].start()
        for j in range(k + 2):
            gram[j, k + 1] = total(sums[j])
    entries = [jnp.broadcast_to(gram[pair], (1, rows)) for pair in PAIRS]
    entries += [jnp.broadcast_to(scale, (1, rows)) for scale in scales]
    entries.append(jnp.zeros((stats_ref.shape[1] - len(entries), rows), F32))
    stats = jnp.concatenate(entries, axis=0)
    for s in range(stats_ref.shape[0]):
        stats_ref[s] = stats
    stores.append(pltpu.make_async_copy(stats_ref, stats_hbm, image_sems.at[ITERS]))
    stores[ITERS].start()
    for store in stores:
        store.wait()


def final_kernel(shift_ref, size_ref, stats_ref, psi_ref, image_ref, out_ref, energy_ref):
    q = lax.axis_index("sector")
    sectors, _, rows = stats_ref.shape
    states = psi_ref.shape[0]
    gram = {}
    for n, (i, j) in enumerate(PAIRS):
        gram[i, j] = gram[j, i] = stats_ref[:, n, :]
    scales = [stats_ref[:, len(PAIRS) + j, :] for j in range(ITERS)]

    def product(a, b):
        total = None
        for i, x in enumerate(a):
            for j, y in enumerate(b):
                if x is not None and y is not None:
                    term = x * y * gram[i, j]
                    total = term if total is None else total + term
        return jnp.sum(total, axis=0, keepdims=True)

    coefs = [jnp.ones((sectors, rows), F32)]
    rayleigh = None
    for _ in range(ITERS):
        image = [None] + [c / s for c, s in zip(coefs, scales)]
        rayleigh = product(coefs, image) / product(coefs, coefs)
        updated = []
        for j in range(len(coefs) + 1):
            value = 0.0
            if j < len(coefs):
                value = (1.0 + STEP * rayleigh) * coefs[j]
            if image[j] is not None:
                value = value - STEP * image[j]
            updated.append(value)
        norm = lax.rsqrt(product(updated, updated))
        coefs = [c * norm for c in updated]
    energy_ref[0] = rayleigh[0, 0]
    sector_id = lax.broadcasted_iota(jnp.int32, (sectors, rows), 0)
    own = [jnp.sum(jnp.where(sector_id == q, c, 0.0), axis=0, keepdims=True) for c in coefs]
    row_id = lax.broadcasted_iota(jnp.int32, (rows, rows), 0)
    col_id = lax.broadcasted_iota(jnp.int32, (rows, rows), 1)
    own_size = size_ref[q]
    for p in range(states):
        limit = slot_limit(q, shift_ref[0, p], size_ref)
        live = jnp.logical_and(col_id < limit, row_id < own_size)
        total = own[0] * jnp.where(live, psi_ref[p].astype(F32), 0.0)
        for k in range(ITERS):
            total = total + own[k + 1] * image_ref[k, p].astype(F32)
        out_ref[p] = total.astype(BF16)


def body(
    left_edge, transfer, completed, right_env, psi_init, mpo, mpo_mask, charge_shift, block_size
):
    channels, rows = left_edge.shape[1:3]
    segments, sectors = lax.axis_size("chain"), lax.axis_size("sector")
    states = psi_init.shape[2]
    slots = 16
    deep = channels * states
    own, psi = right_env[0, 0], psi_init[0, 0]
    operator = jnp.transpose(mpo, (0, 3, 1, 2))

    def kernel(function, out_shape, in_specs, scratch, out_specs=None, flops=0, mib=63, grid=()):
        shapes = out_shape if isinstance(out_shape, tuple) else (out_shape,)
        specs = out_specs or tuple(VMEM_SPEC for _ in shapes)
        return pl.pallas_call(
            function,
            grid=grid,
            out_shape=out_shape,
            in_specs=in_specs,
            out_specs=specs if isinstance(out_shape, tuple) else specs[0],
            scratch_shapes=scratch,
            compiler_params=pltpu.CompilerParams(vmem_limit_bytes=mib * 2**20),
            cost_estimate=pl.CostEstimate(
                flops=flops, bytes_accessed=4 * 2**20, transcendentals=0
            ),
        )

    def shape(*dims, dtype=BF16):
        return jax.ShapeDtypeStruct(dims, dtype)

    payload = kernel(
        pack_kernel,
        shape(segments, 2 * rows, rows),
        [HBM_SPEC] * 2,
        [
            pltpu.VMEM((channels, rows, rows), F32),
            pltpu.VMEM((rows, rows), F32),
            pltpu.VMEM((segments, 2 * rows, rows), BF16),
            pltpu.SemaphoreType.DMA((8,)),
            pltpu.SemaphoreType.DMA((8,)),
        ],
        out_specs=(HBM_SPEC,),
        flops=10**6,
    )(completed[0, 0], transfer[0, 0])
    below = lax.ppermute(own, "sector", [(i, i + 1) for i in range(sectors - 1)])
    above = lax.ppermute(own, "sector", [(i + 1, i) for i in range(sectors - 1)])
    got = lax.all_to_all(payload, "chain", 0, 0, tiled=True)
    env_out = kernel(
        scan_kernel,
        shape(segments, rows, rows),
        [HBM_SPEC] * 2,
        [
            pltpu.VMEM((rows, rows), F32),
            pltpu.VMEM((segments, 2 * rows, rows), BF16),
            pltpu.SemaphoreType.DMA,
            pltpu.SemaphoreType.DMA((4,)),
        ],
        flops=2 * 10**9,
        mib=40,
    )(got, left_edge[0])
    env_out, early = lax.optimization_barrier((env_out, psi))
    env = lax.all_to_all(env_out, "chain", 0, 0, tiled=True)
    wide, mix, start, pairs = kernel(
        prepare_kernel,
        (
            shape(3, rows, rows * slots),
            shape(states * slots, deep),
            shape(rows * states, rows),
            shape(3, states, dtype=jnp.int32),
        ),
        [SMEM_SPEC] * 2 + [VMEM_SPEC] * 6,
        [
            pltpu.VMEM((3, rows * slots, rows), F32),
            pltpu.VMEM((rows * states, rows), F32),
            pltpu.SMEM((3,), jnp.int32),
        ],
        out_specs=(VMEM_SPEC,) * 3 + (SMEM_SPEC,),
        flops=5 * 10**9,
        mib=40,
    )(charge_shift, block_size, below, own, above, early, operator, mpo_mask)
    chunk = 64
    stats, image = kernel(
        ham_kernel,
        (shape(sectors, 16, rows, dtype=F32), shape(ITERS, states, rows, rows)),
        [SMEM_SPEC] * 3 + [VMEM_SPEC] * 3 + [HBM_SPEC] * 2,
        [
            pltpu.VMEM((sectors, 16, rows), F32),
            pltpu.VMEM((ITERS + 1, 8, rows), F32),
            pltpu.VMEM((rows * states, rows), F32),
            pltpu.VMEM((rows * states, rows), BF16),
            pltpu.VMEM((rows, channels * rows), BF16),
            pltpu.VMEM((chunk, deep, rows), BF16),
            pltpu.VMEM((states, rows * slots, rows), BF16),
            pltpu.VMEM((states, rows, rows), BF16),
            pltpu.VMEM((3, rows, rows * slots), BF16),
            pltpu.VMEM((ITERS, states, rows, rows), BF16),
            pltpu.SemaphoreType.DMA((2,)),
            pltpu.SemaphoreType.DMA((ITERS + 1,)),
        ],
        out_specs=(HBM_SPEC, HBM_SPEC),
        flops=10**10,
        mib=40,
    )(charge_shift, block_size, pairs, env, mix, start, psi, wide)
    stats = lax.all_to_all(stats, "sector", 0, 0, tiled=True)
    out, energy = kernel(
        final_kernel,
        (shape(states, rows, rows), shape(1, dtype=F32)),
        [SMEM_SPEC] * 2 + [VMEM_SPEC] * 3,
        [],
        out_specs=(VMEM_SPEC, SMEM_SPEC),
        flops=10**7,
        mib=16,
    )(charge_shift, block_size, stats, psi, image)
    return out[None, None], energy


def solution(mesh):
    placed = (
        P("sector", None, None, None),
        P("chain", "sector", None, None),
        P("chain", "sector", None, None, None),
        P("chain", "sector", None, None, None),
        P("chain", "sector", None, None, None),
        P(),
        P(),
        P("sector", None),
        P(),
    )
    return jax.shard_map(
        body,
        mesh=mesh,
        in_specs=placed,
        out_specs=(P("chain", "sector", None, None, None), P("chain")),
        check_vma=False,
    )
```
